32 devices in a mesh: fsdp: 4 (over z), seq: 8 (over y, x, core).
Axes of the slice: x: 2, y: 2, z: 4, core: 2. Of those that a mesh axis runs over, the one named last changes fastest.
Arguments:
- query_teacher: bfloat16 [4, 1024, 4096], P('fsdp', 'seq'), may hold values from -180 to 180
- key_teacher: bfloat16 [4, 1024, 4096], P('fsdp', 'seq'), may hold values from -180 to 180
- value_teacher: bfloat16 [4, 1024, 4096], P('fsdp', 'seq'), may hold values from -36 to 36
- query_student: bfloat16 [4, 1024, 4096], P('fsdp', 'seq'), may hold values from -180 to 180
- key_student: bfloat16 [4, 1024, 4096], P('fsdp', 'seq'), may hold values from -180 to 180
- value_student: bfloat16 [4, 1024, 4096], P('fsdp', 'seq'), may hold values from -36 to 36
- timesteps: int32 [4], P('fsdp'), may hold values from 0 to 49
- student_gain: float32 [2, 4096], P(None, 'fsdp'), may hold values from 0.1 to 1.9
- ema_gain: float32 [2, 4096], P(None, 'fsdp'), may hold values from 0.1 to 1.9
Outputs:
- student_out: bfloat16 [4, 1024, 4096], P('fsdp', 'seq')
- clip_loss: float32 [4], P('fsdp')
- gain_grad: float32 [2, 4096], P(None, 'fsdp')
- new_student: float32 [2, 4096], P(None, 'fsdp')
- new_ema: float32 [2, 4096], replicated
The draws below stay inside these ranges and needn't reach their ends.
All inputs are finite; a program needn't handle non-finite values.
Results may differ from the reference program's by a relative error of at most 0.019.
The reference program's roundings to bfloat16 on the way count: a program that leaves them out, or rounds other values in their place, can miss the bound.
Values may be sent and summed in bfloat16 or wider, within the bound.
No kernel may reach another device: no remote copies, remote signals or barrier semaphores. Data moves between devices by JAX's collectives and lax.ppermute only.
A program may use at most 128 MiB of HBM per device.

```python
import jax
import jax.numpy as jnp
from jax import lax

HEADS = 32
HEAD_DIM = 128
TSTEPS = 50
INNER = 4096
SEQLEN = 1024
CLIPS = 4


def fresh_rows(key):
    return jnp.clip(jax.random.normal(key, (CLIPS, SEQLEN, INNER), jnp.float32), -6.0, 6.0)


def pre_norm(key, shared_salt, own_salt, mixed):
    values = fresh_rows(jax.random.fold_in(key, shared_salt))
    if mixed:
        values = 0.8 * values + 0.6 * fresh_rows(jax.random.fold_in(key, own_salt))
    return values


def query_rows(key, shared_salt, own_salt, mixed):
    values = pre_norm(key, shared_salt, own_salt, mixed)
    return values.astype(jnp.bfloat16)


def key_rows(key, shared_salt, own_salt, mixed):
    values = pre_norm(key, shared_salt, own_salt, mixed)
    return values.astype(jnp.bfloat16)


def value_noise(key):
    return jnp.clip(6.0 * jax.random.normal(key, (CLIPS, SEQLEN, INNER), jnp.float32), -36.0, 36.0)


def value_rows(key, own_salt, mixed):
    values = value_noise(jax.random.fold_in(key, 31))
    if mixed:
        values = 0.8 * values + 0.6 * value_noise(jax.random.fold_in(key, own_salt))
    return jnp.clip(values, -36.0, 36.0).astype(jnp.bfloat16)


def draw_query_teacher(key, part):
    return query_rows(key, 21, 21, False)


def draw_key_teacher(key, part):
    return key_rows(key, 22, 22, False)


def draw_value_teacher(key, part):
    return value_rows(key, 31, False)


def draw_query_student(key, part):
    return query_rows(key, 21, 23, True)


def draw_key_student(key, part):
    return key_rows(key, 22, 24, True)


def draw_value_student(key, part):
    return value_rows(key, 32, True)


def set_ends(values, rng, smallest, largest):
    extent = values.shape
    index_at = [jax.random.randint(jax.random.fold_in(rng, axis), (), 0, extent[axis]) for axis in range(len(extent))]
    values = values.at[tuple(index_at)].set(smallest)
    longest = extent.index(max(extent))
    index_at[longest] = (index_at[longest] + 1) % extent[longest]
    return values.at[tuple(index_at)].set(largest)


def setup_inputs(seed: int = 0) -> dict:
    key_of = jax.random.split(jax.random.key(seed), 10)
    query_teacher = draw_query_teacher(jax.random.fold_in(key_of[9], 71), 0)
    key_teacher = draw_key_teacher(jax.random.fold_in(key_of[9], 71), 0)
    value_teacher = draw_value_teacher(jax.random.fold_in(key_of[9], 71), 0)
    query_student = draw_query_student(jax.random.fold_in(key_of[9], 71), 0)
    key_student = draw_key_student(jax.random.fold_in(key_of[9], 71), 0)
    value_student = draw_value_student(jax.random.fold_in(key_of[9], 71), 0)
    timesteps = set_ends(jax.random.randint(key_of[6], (CLIPS,), 0, TSTEPS), jax.random.fold_in(key_of[6], 1), 0, TSTEPS - 1).astype(jnp.int32)
    student_gain = jnp.clip(1.0 + 0.18 * jax.random.normal(key_of[7], (2, INNER), jnp.float32), 0.1, 1.9)
    ema_gain = jnp.clip(1.0 + 0.18 * jax.random.normal(key_of[8], (2, INNER), jnp.float32), 0.1, 1.9)
    return {"query_teacher": query_teacher, "key_teacher": key_teacher, "value_teacher": value_teacher, "query_student": query_student, "key_student": key_student, "value_student": value_student, "timesteps": timesteps, "student_gain": student_gain, "ema_gain": ema_gain}


norm_eps = 1e-06
step_size = 0.01
ema_decay = 0.95

def unit_rows(values):
    wide = values.astype(jnp.float32)
    return (wide * lax.rsqrt(lax.optimization_barrier(jnp.mean(wide * wide, axis=-1, keepdims=True)) + norm_eps)).astype(jnp.bfloat16)

def with_gain(unit, gain):
    return (unit.astype(jnp.float32) * gain).astype(jnp.bfloat16)

def softmax_rows(rows, keys, scale):
    scores = jnp.einsum('qgd,kgd->gqk', rows.astype(jnp.float32), keys.astype(jnp.float32)) * scale
    top = lax.optimization_barrier(jnp.max(scores, axis=-1, keepdims=True))
    raised = jnp.exp(scores - top)
    return raised / lax.optimization_barrier(jnp.sum(raised, axis=-1, keepdims=True))

def attend(query, keys, values):
    length = query.shape[0]
    block = min(512, length)
    scale = HEAD_DIM ** (-0.5)
    blocks = query.reshape(length // block, block, query.shape[1], query.shape[2])

    def one(rows):
        weights = softmax_rows(rows, keys, scale).astype(jnp.bfloat16)
        return jnp.einsum('gqk,kgd->qgd', weights.astype(jnp.float32), values.astype(jnp.float32))
    return lax.map(one, blocks).reshape(query.shape)

def backward(query, keys, values, error):
    length = query.shape[0]
    block = min(512, length)
    scale = HEAD_DIM ** (-0.5)
    shape = (length // block, block, query.shape[1], query.shape[2])

    def one(total, parts):
        rows, errs = parts
        probs = softmax_rows(rows, keys, scale)
        dprob = jnp.einsum('qgd,kgd->gqk', errs.astype(jnp.float32), values.astype(jnp.float32))
        dscore = (probs * (dprob - lax.optimization_barrier(jnp.sum(probs * dprob, axis=-1, keepdims=True)))).astype(jnp.bfloat16)
        dquery = (jnp.einsum('gqk,kgd->qgd', dscore.astype(jnp.float32), keys.astype(jnp.float32)) * scale).astype(jnp.bfloat16)
        total = total + jnp.einsum('gqk,qgd->kgd', dscore.astype(jnp.float32), rows.astype(jnp.float32))
        return (total, dquery)
    start = jnp.zeros(keys.shape, jnp.float32)
    total, dquery = lax.scan(one, start, (query.reshape(shape), error.reshape(shape)))
    return (dquery.reshape(query.shape), (total * scale).astype(jnp.bfloat16))

def per_head(function, arrays):
    stacked = tuple((jnp.moveaxis(item, 1, 0)[:, :, None, :] for item in arrays))
    result = lax.map(lambda group: function(*group), stacked)
    return jax.tree.map(lambda item: jnp.moveaxis(item[:, :, 0, :], 0, 1), result)

def reference(query_teacher, key_teacher, value_teacher, query_student, key_student, value_student, timesteps, student_gain, ema_gain):
    weights = 1.0 / (0.05 + (timesteps.astype(jnp.float32) + 1.0) / TSTEPS)

    def split(values):
        return values.reshape(SEQLEN, HEADS, HEAD_DIM)

    def clip_step(parts):
        qt, kt, vt, qs, ks, vs, weight = parts
        unit_qs = unit_rows(qs)
        unit_ks = unit_rows(ks)
        teacher_q = with_gain(unit_rows(qt), ema_gain[0])
        teacher_k = with_gain(unit_rows(kt), ema_gain[1])
        student_q = with_gain(unit_qs, student_gain[0])
        student_k = with_gain(unit_ks, student_gain[1])
        target = per_head(attend, (split(teacher_q), split(teacher_k), split(vt))).astype(jnp.bfloat16)
        output = per_head(attend, (split(student_q), split(student_k), split(vs))).astype(jnp.bfloat16)
        factor = weight / (SEQLEN * HEADS)
        diff = output.astype(jnp.float32) - target.astype(jnp.float32)
        loss = factor * jnp.sum(diff * diff)
        error = (2.0 * factor * diff).astype(jnp.bfloat16)
        dquery, dkey = per_head(backward, (split(student_q), split(student_k), split(vs), error))
        term_q = lax.optimization_barrier(jnp.sum(dquery.reshape(SEQLEN, INNER).astype(jnp.float32) * unit_qs.astype(jnp.float32), axis=0))
        term_k = lax.optimization_barrier(jnp.sum(dkey.reshape(SEQLEN, INNER).astype(jnp.float32) * unit_ks.astype(jnp.float32), axis=0))
        return (output.reshape(SEQLEN, INNER), loss, jnp.stack([term_q, term_k]))
    student_out, clip_loss, terms = lax.map(clip_step, (query_teacher, key_teacher, value_teacher, query_student, key_student, value_student, weights))
    gain_grad = lax.optimization_barrier(jnp.sum(terms, axis=0))
    new_student = student_gain - step_size * gain_grad
    new_ema = ema_decay * ema_gain + (1.0 - ema_decay) * new_student
    return (student_out, clip_loss, gain_grad, new_student, new_ema)
```

```python
import functools
import math

import jax
import jax.numpy as jnp
from jax import lax
from jax.experimental import pallas as pl
from jax.experimental.pallas import tpu as pltpu
from jax.sharding import PartitionSpec as P

HEAD_DIM = 128
TSTEPS = 50

norm_eps = 1e-06
step_size = 0.01
ema_decay = 0.95

VMEM_BYTES = 48 * 1024 * 1024
QUERY_BLOCK = 256

f32 = jnp.float32
bf16 = jnp.bfloat16


def params(limit=VMEM_BYTES):
    return pltpu.CompilerParams(vmem_limit_bytes=limit)


def cost(flops, nbytes, exps=0):
    return pl.CostEstimate(flops=flops, bytes_accessed=nbytes, transcendentals=exps)


def swap(x, axis, step):
    size = lax.axis_size(axis)
    return lax.ppermute(x, axis, [(i, i ^ step) for i in range(size)])


def nt(a, b):
    return lax.dot_general(a, b, (((1,), (1,)), ((), ())), preferred_element_type=f32)


def nn(a, b):
    return lax.dot_general(a, b, (((1,), (0,)), ((), ())), preferred_element_type=f32)


def prep_kernel(groups, width, plans, *refs):
    ins, outs = refs[:3], refs[3:]
    me = lax.axis_index("seq")
    inverse = []
    for x_ref in ins[:2]:
        wide = x_ref[...].astype(f32)
        inverse.append(lax.rsqrt(jnp.mean(wide * wide, axis=-1, keepdims=True) + norm_eps))

    at = 0
    for first, columns, by_step in plans:
        for slot in range(groups):
            if by_step:
                col = pl.multiple_of((me ^ slot) * width + first, HEAD_DIM)
            else:
                col = slot * width + first
            for a in range(3):
                part = ins[a][:, pl.ds(col, columns)]
                if a < 2:
                    part = (part.astype(f32) * inverse[a]).astype(bf16)
                if by_step:
                    outs[at + slot][a] = part
                else:
                    outs[at][slot, a] = part
        at += groups if by_step else 1


def prep(q, k, v, groups, width, plans):
    tokens, inner = q.shape
    rows = min(32, tokens)
    shapes, specs = [], []
    for _, columns, by_step in plans:
        if by_step:
            for _ in range(groups):
                shapes.append(jax.ShapeDtypeStruct((3, tokens, columns), bf16))
                specs.append(pl.BlockSpec((3, rows, columns), lambda i: (0, i, 0)))
        else:
            shapes.append(jax.ShapeDtypeStruct((groups, 3, tokens, columns), bf16))
            specs.append(pl.BlockSpec((groups, 3, rows, columns), lambda i: (0, 0, i, 0)))
    return pl.pallas_call(
        functools.partial(prep_kernel, groups, width, plans),
        grid=(tokens // rows,),
        in_specs=[pl.BlockSpec((rows, inner), lambda i: (i, 0))] * 3,
        out_specs=specs,
        out_shape=shapes,
        compiler_params=params(),
        cost_estimate=cost(20 * tokens * inner, 12 * tokens * inner),
        name="prep",
    )(q, k, v)


def part_at(refs, me, slot, a):
    if len(refs) > 1:
        return refs[slot][a]
    return refs[0][me ^ slot, a]


def load(refs, me, groups, tokens, gains, q_scr, k_scr, v_scr):
    for slot in range(groups):
        rows = pl.ds(slot * tokens, tokens)
        q_scr[rows, :] = (part_at(refs, me, slot, 0).astype(f32) * gains[0]).astype(bf16)
        k_scr[rows, :] = (part_at(refs, me, slot, 1).astype(f32) * gains[1]).astype(bf16)
        v_scr[rows, :] = part_at(refs, me, slot, 2)


def head_gains(gain_ref, me, width, column):
    col = pl.multiple_of(me * width + column, HEAD_DIM)
    return gain_ref[:, pl.ds(col, HEAD_DIM)]


def probabilities(q, k):
    factor = HEAD_DIM ** (-0.5) * math.log2(math.e)
    scores = nt(q, k)
    top = jnp.max(scores, axis=-1, keepdims=True)
    raised = jnp.exp2((scores - top) * factor)
    total = jnp.sum(raised, axis=-1, keepdims=True)
    return raised * (1.0 / total), top * factor + jnp.log2(total)


def student_kernel(groups, tokens, width, n_in, *refs):
    ins = refs[:n_in]
    gain_ref, out_ref, lse_ref, q_scr, k_scr, v_scr = refs[n_in:]
    me = lax.axis_index("seq")
    gains = head_gains(gain_ref, me, width, pl.program_id(0) * HEAD_DIM)
    load(ins, me, groups, tokens, (gains[0:1], gains[1:2]), q_scr, k_scr, v_scr)
    length = groups * tokens
    block = min(QUERY_BLOCK, length)
    for start in range(0, length, block):
        rows = pl.ds(start, block)
        probs, lse = probabilities(q_scr[rows, :], k_scr[...])
        out = nn(probs.astype(bf16), v_scr[...]).astype(bf16)
        lse_ref[0, rows, :] = jnp.broadcast_to(lse, (block, HEAD_DIM))
        for j in range(block // tokens):
            out_ref[me ^ (start // tokens + j)] = out[j * tokens : (j + 1) * tokens]


def chunk_specs(arrays, groups, tokens, first):
    if len(arrays) > 1:
        return [pl.BlockSpec((3, tokens, HEAD_DIM), lambda h: (0, 0, first + h))] * groups
    return [pl.BlockSpec((groups, 3, tokens, HEAD_DIM), lambda h: (0, 0, 0, first + h))]


def student(arrays, gains, groups, tokens, width):
    heads = width // HEAD_DIM
    length = groups * tokens
    work = length * length * heads
    return pl.pallas_call(
        functools.partial(student_kernel, groups, tokens, width, len(arrays)),
        grid=(heads,),
        in_specs=chunk_specs(arrays, groups, tokens, 0) + [pl.BlockSpec(gains.shape, lambda h: (0, 0))],
        out_specs=[
            pl.BlockSpec((groups, tokens, HEAD_DIM), lambda h: (0, 0, h)),
            pl.BlockSpec((1, length, HEAD_DIM), lambda h: (h, 0, 0)),
        ],
        out_shape=[
            jax.ShapeDtypeStruct((groups, tokens, width), bf16),
            jax.ShapeDtypeStruct((heads, length, HEAD_DIM), f32),
        ],
        scratch_shapes=[pltpu.VMEM((length, HEAD_DIM), bf16)] * 3,
        compiler_params=params(),
        cost_estimate=cost(8 * HEAD_DIM * work, 8 * length * width, work),
        name="student",
    )(*arrays, gains)


def teacher_kernel(groups, tokens, width, first, n_teacher, n_student, has_before, *refs):
    step_ref, *refs = refs
    teacher_refs, refs = refs[:n_teacher], refs[n_teacher:]
    student_refs, refs = refs[:n_student], refs[n_student:]
    gain_ref, out_ref, lse_ref, *refs = refs
    if has_before:
        before_ref, *refs = refs
    grad_ref, qt, kt, vt, qs, ks, vs = refs
    length = groups * tokens
    block = min(QUERY_BLOCK, length)
    scale = HEAD_DIM ** (-0.5)
    factor = scale * math.log2(math.e)
    head = pl.program_id(0)
    me = lax.axis_index("seq")
    column = (first + head) * HEAD_DIM
    gains = head_gains(gain_ref, me, width, column)
    load(teacher_refs, me, groups, tokens, (gains[2:3], gains[3:4]), qt, kt, vt)
    load(student_refs, me, groups, tokens, (gains[0:1], gains[1:2]), qs, ks, vs)
    step = jnp.full((1, HEAD_DIM), step_ref[0], jnp.int32).astype(f32)
    weight = 1.0 / (0.05 + (step + 1.0) / TSTEPS)
    share = weight / (length * (groups * width // HEAD_DIM))

    if has_before:

        @pl.when(head == 0)
        def _():
            grad_ref[...] = before_ref[...]

    else:

        @pl.when(head == 0)
        def _():
            grad_ref[...] = jnp.zeros_like(grad_ref)

    squares = jnp.zeros((1, HEAD_DIM), f32)
    term_q = jnp.zeros((1, HEAD_DIM), f32)
    key_grad = None
    for start in range(0, length, block):
        rows = pl.ds(start, block)
        slots = range(start // tokens, start // tokens + block // tokens)
        probs, _ = probabilities(qt[rows, :], kt[...])
        target = nn(probs.astype(bf16), vt[...]).astype(bf16)
        out = jnp.concatenate([out_ref[me ^ slot] for slot in slots], axis=0)
        diff = out.astype(f32) - target.astype(f32)
        squares = squares + jnp.sum(diff * diff, axis=0, keepdims=True)
        error = (2.0 * share * diff).astype(bf16)
        lse = lse_ref[0, rows, :][:, :1]
        probs = jnp.exp2(nt(qs[rows, :], ks[...]) * factor - lse)
        dprob = nt(error, vs[...])
        inner = jnp.sum(probs * dprob, axis=-1, keepdims=True)
        dscore = (probs * (dprob - inner)).astype(bf16)
        dquery = (nn(dscore, ks[...]) * scale).astype(bf16)
        unit = jnp.concatenate([part_at(student_refs, me, slot, 0) for slot in slots], axis=0)
        term_q = term_q + jnp.sum(dquery.astype(f32) * unit.astype(f32), axis=0, keepdims=True)
        part = nn(jnp.transpose(qs[rows, :]), dscore)
        key_grad = part if key_grad is None else key_grad + part
    dkey = (jnp.transpose(key_grad) * scale).astype(bf16)
    unit = jnp.concatenate([part_at(student_refs, me, slot, 1) for slot in range(groups)], axis=0)
    term_k = jnp.sum(dkey.astype(f32) * unit.astype(f32), axis=0, keepdims=True)
    cols = pl.ds(pl.multiple_of(column, HEAD_DIM), HEAD_DIM)
    grad_ref[0:1, cols] = term_q
    grad_ref[1:2, cols] = term_k
    grad_ref[2:3, cols] = share * squares


def teacher(timesteps, arrays, student_arrays, gains, out, lse, before, first, heads, groups, tokens, width):
    length = groups * tokens
    work = length * length * heads
    extra = [] if before is None else [before]
    return pl.pallas_call(
        functools.partial(
            teacher_kernel, groups, tokens, width, first, len(arrays), len(student_arrays), before is not None
        ),
        grid=(heads,),
        in_specs=[pl.BlockSpec(memory_space=pltpu.SMEM)]
        + chunk_specs(arrays, groups, tokens, 0)
        + chunk_specs(student_arrays, groups, tokens, first)
        + [
            pl.BlockSpec(gains.shape, lambda h: (0, 0)),
            pl.BlockSpec((groups, tokens, HEAD_DIM), lambda h: (0, 0, first + h)),
            pl.BlockSpec((1, length, HEAD_DIM), lambda h: (first + h, 0, 0)),
        ]
        + [pl.BlockSpec((8, width), lambda h: (0, 0))] * len(extra),
        out_specs=pl.BlockSpec((8, width), lambda h: (0, 0)),
        out_shape=jax.ShapeDtypeStruct((8, width), f32),
        scratch_shapes=[pltpu.VMEM((length, HEAD_DIM), bf16)] * 6,
        compiler_params=params(),
        cost_estimate=cost(24 * HEAD_DIM * work, 16 * length * heads * HEAD_DIM, 2 * work),
        name="teacher",
    )(timesteps, *arrays, *student_arrays, gains, out, lse, *extra)


def sum_kernel(n, groups, *refs):
    ins, out_ref = refs[:n], refs[n]
    parts = [ref[0:2, :] for ref in ins]
    while len(parts) > 1:
        parts = [parts[i] + parts[i + 1] for i in range(0, len(parts), 2)]
    for j in range(groups):
        out_ref[j, 0:2, :] = parts[0]
        out_ref[j, 2:, :] = ins[0][2:, :]


def clip_sum(parts, groups):
    rows, width = parts[0].shape
    return pl.pallas_call(
        functools.partial(sum_kernel, len(parts), groups),
        out_shape=jax.ShapeDtypeStruct((groups, rows, width), f32),
        name="clip_sum",
    )(*parts)


def final_kernel(groups, width, own, terms_ref, gain_ref, loss_ref, grad_ref, student_ref, ema_ref):
    loss = jnp.zeros((1, width), f32)
    for j in range(groups):
        cols = pl.ds(j * width, width)
        term = terms_ref[j, 0:2, :]
        loss = loss + terms_ref[j, 2:3, :]
        new = gain_ref[0:2, cols] - step_size * term
        ema_ref[:, cols] = ema_decay * gain_ref[2:4, cols] + (1.0 - ema_decay) * new
    loss_ref[0] = jnp.sum(loss)
    for z in range(groups * width // own):

        @pl.when(lax.axis_index("fsdp") == z)
        def _():
            for j in range(groups):
                low, high = max(j * width, z * own), min((j + 1) * width, (z + 1) * own)
                if low < high:
                    term = terms_ref[j, 0:2, low - j * width : high - j * width]
                    grad_ref[:, low - z * own : high - z * own] = term
                    student_ref[:, low - z * own : high - z * own] = gain_ref[0:2, low:high] - step_size * term


def finish(terms, gains, own):
    groups, _, width = terms.shape
    return pl.pallas_call(
        functools.partial(final_kernel, groups, width, own),
        out_shape=[
            jax.ShapeDtypeStruct((1,), f32),
            jax.ShapeDtypeStruct((2, own), f32),
            jax.ShapeDtypeStruct((2, own), f32),
            jax.ShapeDtypeStruct((2, groups * width), f32),
        ],
        out_specs=[pl.BlockSpec(memory_space=pltpu.SMEM)] + [pl.BlockSpec(memory_space=pltpu.VMEM)] * 3,
        name="finish",
    )(terms, gains)


def by_step(parts):
    return [parts[0]] + [swap(parts[step], "seq", step) for step in range(1, len(parts))]


def by_source(stacked):
    return [lax.all_to_all(stacked, "seq", split_axis=0, concat_axis=0, tiled=True)]


def local(
    query_teacher,
    key_teacher,
    value_teacher,
    query_student,
    key_student,
    value_student,
    timesteps,
    student_gain,
    ema_gain,
):
    groups = lax.axis_size("seq")
    clips = lax.axis_size("fsdp")
    tokens = query_teacher.shape[1]
    inner = query_teacher.shape[2]
    width = inner // groups
    heads = width // HEAD_DIM
    split = (heads + 1) // 2 * HEAD_DIM

    sent = prep(query_student[0], key_student[0], value_student[0], groups, width, [(0, width, True)])
    student_parts = by_step(sent)
    sent = prep(
        query_teacher[0],
        key_teacher[0],
        value_teacher[0],
        groups,
        width,
        [(0, split, False), (split, width - split, True)],
    )
    teacher_first = by_source(sent[0])
    gains = lax.all_gather(jnp.concatenate([student_gain, ema_gain], axis=0), "fsdp", axis=1, tiled=True)

    out, lse = student(student_parts, gains, groups, tokens, width)
    teacher_second = by_step(sent[1:])
    grads = teacher(
        timesteps, teacher_first, student_parts, gains, out, lse, None, 0, split // HEAD_DIM, groups, tokens, width
    )
    returned = by_source(out)[0]
    grads = teacher(
        timesteps,
        teacher_second,
        student_parts,
        gains,
        out,
        lse,
        grads,
        split // HEAD_DIM,
        heads - split // HEAD_DIM,
        groups,
        tokens,
        width,
    )
    student_out = jnp.moveaxis(returned, 0, 1).reshape(1, tokens, inner)
    terms = clip_sum([grads] + [swap(grads, "fsdp", step) for step in range(1, clips)], groups)
    terms = by_source(terms)[0]
    loss, gain_grad, new_student, new_ema = finish(terms, gains, student_gain.shape[1])
    return (student_out, loss, gain_grad, new_student, new_ema)


def solution(mesh):
    in_specs = (
        P("fsdp", "seq", None),
        P("fsdp", "seq", None),
        P("fsdp", "seq", None),
        P("fsdp", "seq", None),
        P("fsdp", "seq", None),
        P("fsdp", "seq", None),
        P("fsdp"),
        P(None, "fsdp"),
        P(None, "fsdp"),
    )
    out_specs = (P("fsdp", "seq", None), P("fsdp"), P(None, "fsdp"), P(None, "fsdp"), P())
    return jax.shard_map(local, mesh=mesh, in_specs=in_specs, out_specs=out_specs, check_vma=False)
```

```python
import functools
import math

import jax
import jax.numpy as jnp
from jax import lax
from jax.experimental import pallas as pl
from jax.experimental.pallas import tpu as pltpu
from jax.sharding import PartitionSpec as P

HEAD_DIM = 128
TSTEPS = 50

norm_eps = 1e-06
step_size = 0.01
ema_decay = 0.95

VMEM_BYTES = 60 * 1024 * 1024
STUDENT_BLOCK = 512
TEACHER_BLOCK = 512
TERMS = 4

f32 = jnp.float32
bf16 = jnp.bfloat16


def params(limit=VMEM_BYTES):
    return pltpu.CompilerParams(vmem_limit_bytes=limit)


def cost(flops, nbytes, exps=0):
    return pl.CostEstimate(flops=flops, bytes_accessed=nbytes, transcendentals=exps)


def swap(x, axis, step):
    size = lax.axis_size(axis)
    return lax.ppermute(x, axis, [(i, i ^ step) for i in range(size)])


def nn(a, b):
    return lax.dot_general(a, b, (((1,), (0,)), ((), ())), preferred_element_type=f32)


def prep_kernel(groups, width, plans, *refs):
    ins, outs = refs[:3], refs[3:]
    me = lax.axis_index("seq")
    inverse = []
    for x_ref in ins[:2]:
        wide = x_ref[...].astype(f32)
        inverse.append(lax.rsqrt(jnp.mean(wide * wide, axis=-1, keepdims=True) + norm_eps))

    at = 0
    for first, columns, by_step in plans:
        for slot in range(groups):
            if by_step:
                col = pl.multiple_of((me ^ slot) * width + first, HEAD_DIM)
            else:
                col = slot * width + first
            for a in range(3):
                part = ins[a][:, pl.ds(col, columns)]
                if a < 2:
                    part = (part.astype(f32) * inverse[a]).astype(bf16)
                for h in range(columns // HEAD_DIM):
                    head = part[:, h * HEAD_DIM : (h + 1) * HEAD_DIM]
                    if by_step:
                        outs[at + slot][h, a] = head
                    else:
                        outs[at][slot, h, a] = head
        at += groups if by_step else 1


def prep(q, k, v, groups, width, plans):
    tokens, inner = q.shape
    rows = min(32, tokens)
    shapes, specs = [], []
    for _, columns, by_step in plans:
        heads = columns // HEAD_DIM
        if by_step:
            for _ in range(groups):
                shapes.append(jax.ShapeDtypeStruct((heads, 3, tokens, HEAD_DIM), bf16))
                specs.append(pl.BlockSpec((heads, 3, rows, HEAD_DIM), lambda i: (0, 0, i, 0)))
        else:
            shapes.append(jax.ShapeDtypeStruct((groups, heads, 3, tokens, HEAD_DIM), bf16))
            specs.append(pl.BlockSpec((groups, heads, 3, rows, HEAD_DIM), lambda i: (0, 0, 0, i, 0)))
    return pl.pallas_call(
        functools.partial(prep_kernel, groups, width, plans),
        grid=(tokens // rows,),
        in_specs=[pl.BlockSpec((rows, inner), lambda i: (i, 0))] * 3,
        out_specs=specs,
        out_shape=shapes,
        compiler_params=params(),
        cost_estimate=cost(20 * tokens * inner, 12 * tokens * inner),
        name="prep",
    )(q, k, v)


def scales(refs):
    found = []
    for x_ref in refs:
        wide = x_ref[...].astype(f32)
        found.append(lax.rsqrt(jnp.mean(wide * wide, axis=-1, keepdims=True) + norm_eps))
    return found


def unit_part(ins, inverse, a, col):
    part = ins[a][:, pl.ds(col, HEAD_DIM)]
    return (part.astype(f32) * inverse[a]).astype(bf16) if a < 2 else part


def sibling_kernel(groups, width, *refs):
    ins, out_ref = refs[:3], refs[3]
    me = lax.axis_index("seq")
    inverse = scales(ins[:2])
    for pair in range(groups // 2):
        for h in range(width // HEAD_DIM):
            col = pl.multiple_of((me ^ (2 * pair + 1)) * width + h * HEAD_DIM, HEAD_DIM)
            for a in range(3):
                out_ref[pair, h, a] = unit_part(ins, inverse, a, col)


def pair_kernel(groups, width, counts, *refs):
    ins, near_ref, outs = refs[:3], refs[3], refs[4:]
    me = lax.axis_index("seq")
    inverse = scales(ins[:2])
    at = first = 0
    for count in counts:
        for pair in range(groups // 2):
            for h in range(count):
                col = pl.multiple_of((me ^ (2 * pair)) * width + (first + h) * HEAD_DIM, HEAD_DIM)
                for a in range(3):
                    outs[at + pair][0, h, a] = unit_part(ins, inverse, a, col)
                    outs[at + pair][1, h, a] = near_ref[pair, first + h, a]
        at += groups // 2
        first += count


def prep_pairs(q, k, v, groups, width, counts, near):
    tokens, inner = q.shape
    heads = width // HEAD_DIM
    rows = min(32, tokens)
    in_specs = [pl.BlockSpec((rows, inner), lambda i: (i, 0))] * 3
    near_spec = pl.BlockSpec((groups // 2, heads, 3, rows, HEAD_DIM), lambda i: (0, 0, 0, i, 0))
    near_shape = jax.ShapeDtypeStruct((groups // 2, heads, 3, tokens, HEAD_DIM), bf16)
    if near is None:
        return pl.pallas_call(
            functools.partial(sibling_kernel, groups, width),
            grid=(tokens // rows,),
            in_specs=in_specs,
            out_specs=near_spec,
            out_shape=near_shape,
            compiler_params=params(),
            cost_estimate=cost(20 * tokens * inner, 9 * tokens * inner),
            name="prep_near",
        )(q, k, v)
    shapes, specs = [], []
    for count in counts:
        for _ in range(groups // 2):
            shapes.append(jax.ShapeDtypeStruct((2, count, 3, tokens, HEAD_DIM), bf16))
            specs.append(pl.BlockSpec((2, count, 3, rows, HEAD_DIM), lambda i: (0, 0, 0, i, 0)))
    return pl.pallas_call(
        functools.partial(pair_kernel, groups, width, counts),
        grid=(tokens // rows,),
        in_specs=in_specs + [near_spec],
        out_specs=specs,
        out_shape=shapes,
        compiler_params=params(),
        cost_estimate=cost(20 * tokens * inner, 15 * tokens * inner),
        name="prep_pairs",
    )(q, k, v, near)


def part_at(refs, me, slot, a):
    if refs[0].ndim == 5:
        return refs[slot // 2][slot % 2, 0, a]
    return refs[slot][0, a]


def head_gains(gain_ref, me, width, column):
    own = gain_ref.shape[2]
    tile = (me * width + column) // HEAD_DIM
    tiles = own // HEAD_DIM
    col = pl.multiple_of(lax.rem(tile, tiles) * HEAD_DIM, HEAD_DIM)
    return gain_ref[tile // tiles, :, pl.ds(col, HEAD_DIM)]


def with_gain(unit, gain):
    return (unit.astype(f32) * gain).astype(bf16)


def nt(a, b):
    return lax.dot_general(a, b, (((1,), (1,)), ((), ())), preferred_element_type=f32)


def load(refs, me, groups, tokens, gains, q_scr, k_scr, v_scr):
    for slot in range(groups):
        rows = pl.ds(slot * tokens, tokens)
        q_scr[rows, :] = with_gain(part_at(refs, me, slot, 0), gains[0])
        k_scr[rows, :] = with_gain(part_at(refs, me, slot, 1), gains[1])
        v_scr[rows, :] = part_at(refs, me, slot, 2)


def probabilities(scores):
    factor = HEAD_DIM ** (-0.5) * math.log2(math.e)
    top = jnp.max(scores, axis=-1, keepdims=True)
    raised = jnp.exp2((scores - top) * factor)
    total = jnp.sum(raised, axis=-1, keepdims=True)
    return raised * (1.0 / total), top * factor + jnp.log2(total)


def student_kernel(groups, tokens, width, n_in, *refs):
    ins = refs[:n_in]
    gain_ref, out_ref, lse_ref, q_scr, k_scr, v_scr = refs[n_in:]
    me = lax.axis_index("seq")
    gains = head_gains(gain_ref, me, width, pl.program_id(0) * HEAD_DIM)
    load(ins, me, groups, tokens, (gains[0:1], gains[1:2]), q_scr, k_scr, v_scr)
    length = groups * tokens
    block = min(STUDENT_BLOCK, length)
    scores = nt(q_scr[0:block, :], k_scr[...])
    for start in range(0, length, block):
        rows = pl.ds(start, block)
        later = start + block
        following = nt(q_scr[later : later + block, :], k_scr[...]) if later < length else None
        probs, lse = probabilities(scores)
        scores = following
        out = nn(probs.astype(bf16), v_scr[...]).astype(bf16)
        lse_ref[0, rows, :] = jnp.broadcast_to(lse, (block, HEAD_DIM))
        for j in range(block // tokens):
            out_ref[me ^ (start // tokens + j), 0] = out[j * tokens : (j + 1) * tokens]


def chunk_specs(arrays, groups, tokens, first):
    if arrays[0].ndim == 5:
        return [pl.BlockSpec((2, 1, 3, tokens, HEAD_DIM), lambda h: (0, first + h, 0, 0, 0))] * len(arrays)
    return [pl.BlockSpec((1, 3, tokens, HEAD_DIM), lambda h: (first + h, 0, 0, 0))] * groups


def student(arrays, gains, groups, tokens, width):
    heads = width // HEAD_DIM
    length = groups * tokens
    work = length * length * heads
    return pl.pallas_call(
        functools.partial(student_kernel, groups, tokens, width, len(arrays)),
        grid=(heads,),
        in_specs=chunk_specs(arrays, groups, tokens, 0) + [pl.BlockSpec(gains.shape, lambda h: (0, 0, 0))],
        out_specs=[
            pl.BlockSpec((groups, 1, tokens, HEAD_DIM), lambda h: (0, h, 0, 0)),
            pl.BlockSpec((1, length, HEAD_DIM), lambda h: (h, 0, 0)),
        ],
        out_shape=[
            jax.ShapeDtypeStruct((groups, heads, tokens, HEAD_DIM), bf16),
            jax.ShapeDtypeStruct((heads, length, HEAD_DIM), f32),
        ],
        scratch_shapes=[pltpu.VMEM((length, HEAD_DIM), bf16)] * 3,
        compiler_params=params(),
        cost_estimate=cost(8 * HEAD_DIM * work, 8 * length * width, work),
        name="student",
    )(*arrays, gains)


def teacher_kernel(groups, tokens, width, first, n_teacher, n_student, has_before, *refs):
    step_ref, *refs = refs
    teacher_refs, refs = refs[:n_teacher], refs[n_teacher:]
    student_refs, refs = refs[:n_student], refs[n_student:]
    gain_ref, out_ref, lse_ref, *refs = refs
    if has_before:
        before_ref, *refs = refs
    all_ref, grad_ref, qt, kt, vt, qs, ks, vs = refs
    length = groups * tokens
    block = min(TEACHER_BLOCK, length)
    scale = HEAD_DIM ** (-0.5)
    factor = scale * math.log2(math.e)
    head = pl.program_id(0)
    me = lax.axis_index("seq")
    column = (first + head) * HEAD_DIM
    gains = head_gains(gain_ref, me, width, column)
    load(teacher_refs, me, groups, tokens, (gains[2:3], gains[3:4]), qt, kt, vt)
    load(student_refs, me, groups, tokens, (gains[0:1], gains[1:2]), qs, ks, vs)
    step = jnp.full((1, HEAD_DIM), step_ref[0], jnp.int32).astype(f32)
    weight = 1.0 / (0.05 + (step + 1.0) / TSTEPS)
    share = weight / (length * (groups * width // HEAD_DIM))

    @pl.when(head == 0)
    def _():
        grad_ref[...] = before_ref[...] if has_before else jnp.zeros_like(grad_ref)

    squares = jnp.zeros((1, HEAD_DIM), f32)
    term_q = jnp.zeros((1, HEAD_DIM), f32)
    key_grad = None
    for start in range(0, length, block):
        rows = pl.ds(start, block)
        slots = range(start // tokens, start // tokens + block // tokens)
        scores = nt(qt[rows, :], kt[...])
        student_scores = nt(qs[rows, :], ks[...])
        probs, _ = probabilities(scores)
        target = nn(probs.astype(bf16), vt[...]).astype(bf16)
        out = jnp.concatenate([out_ref[me ^ slot, 0] for slot in slots], axis=0)
        diff = out.astype(f32) - target.astype(f32)
        squares = squares + jnp.sum(diff * diff, axis=0, keepdims=True)
        error = (2.0 * share * diff).astype(bf16)
        dprob = nt(error, vs[...])
        lse = jnp.concatenate([lse_ref[0, rows, :]] * (length // HEAD_DIM), axis=1)
        probs = jnp.exp2(student_scores * factor - lse)
        inner = jnp.sum(probs * dprob, axis=-1, keepdims=True)
        dscore = (probs * (dprob - inner)).astype(bf16)
        dquery = (nn(dscore, ks[...]) * scale).astype(bf16)
        unit = jnp.concatenate([part_at(student_refs, me, slot, 0) for slot in slots], axis=0)
        term_q = term_q + jnp.sum(dquery.astype(f32) * unit.astype(f32), axis=0, keepdims=True)
        part = nn(jnp.transpose(qs[rows, :]), dscore)
        key_grad = part if key_grad is None else key_grad + part
    dkey = (jnp.transpose(key_grad) * scale).astype(bf16)
    unit = jnp.concatenate([part_at(student_refs, me, slot, 1) for slot in range(groups)], axis=0)
    term_k = jnp.sum(dkey.astype(f32) * unit.astype(f32), axis=0, keepdims=True)
    cols = pl.ds(pl.multiple_of(column, HEAD_DIM), HEAD_DIM)
    grad_ref[0:1, cols] = term_q
    grad_ref[1:2, cols] = term_k
    grad_ref[2:3, cols] = share * squares

    @pl.when(head == pl.num_programs(0) - 1)
    def _():
        for copy in range(all_ref.shape[0]):
            all_ref[copy] = grad_ref[...]


def teacher(timesteps, arrays, student_arrays, gains, out, lse, before, first, heads, groups, tokens, width, copies):
    length = groups * tokens
    work = length * length * heads
    extra = [] if before is None else [before]
    return pl.pallas_call(
        functools.partial(
            teacher_kernel, groups, tokens, width, first, len(arrays), len(student_arrays), before is not None
        ),
        grid=(heads,),
        in_specs=[pl.BlockSpec(memory_space=pltpu.SMEM)]
        + chunk_specs(arrays, groups, tokens, 0)
        + chunk_specs(student_arrays, groups, tokens, first)
        + [
            pl.BlockSpec(gains.shape, lambda h: (0, 0, 0)),
            pl.BlockSpec((groups, 1, tokens, HEAD_DIM), lambda h: (0, first + h, 0, 0)),
            pl.BlockSpec((1, length, HEAD_DIM), lambda h: (first + h, 0, 0)),
        ]
        + [pl.BlockSpec((None, TERMS, width), lambda h: (0, 0, 0))] * len(extra),
        out_specs=pl.BlockSpec((copies, TERMS, width), lambda h: (0, 0, 0)),
        out_shape=jax.ShapeDtypeStruct((copies, TERMS, width), f32),
        scratch_shapes=[pltpu.VMEM((TERMS, width), f32)] + [pltpu.VMEM((length, HEAD_DIM), bf16)] * 6,
        compiler_params=params(),
        cost_estimate=cost(24 * HEAD_DIM * work, 16 * length * heads * HEAD_DIM, 2 * work),
        name="teacher",
    )(timesteps, *arrays, *student_arrays, gains, out, lse, *extra)


def final_kernel(clips, groups, width, own, terms_ref, gain_ref, loss_ref, grad_ref, student_ref, ema_ref):
    clip = lax.axis_index("fsdp")
    loss = jnp.zeros((1, width), f32)
    terms = []
    for j in range(groups):
        term = terms_ref[j, 0:2, :]
        for other in range(1, clips):
            term = term + terms_ref[other * groups + j, 0:2, :]
        terms.append(term)
        loss = loss + terms_ref[clip * groups + j, 2:3, :]
    loss_ref[0] = jnp.sum(loss)
    for z in range(clips):
        pieces = []
        for j in range(groups):
            low, high = max(j * width, z * own), min((j + 1) * width, (z + 1) * own)
            if low < high:
                pieces.append(terms[j][:, low - j * width : high - j * width])
        term = jnp.concatenate(pieces, axis=1)
        new = gain_ref[z, 0:2, :] - step_size * term
        ema_ref[:, z * own : (z + 1) * own] = ema_decay * gain_ref[z, 2:4, :] + (1.0 - ema_decay) * new

        @pl.when(clip == z)
        def _():
            grad_ref[...] = term
            student_ref[...] = new


def finish(terms, gains, groups, own):
    devices, _, width = terms.shape
    return pl.pallas_call(
        functools.partial(final_kernel, devices // groups, groups, width, own),
        out_shape=[
            jax.ShapeDtypeStruct((1,), f32),
            jax.ShapeDtypeStruct((2, own), f32),
            jax.ShapeDtypeStruct((2, own), f32),
            jax.ShapeDtypeStruct((2, groups * width), f32),
        ],
        out_specs=[pl.BlockSpec(memory_space=pltpu.SMEM)] + [pl.BlockSpec(memory_space=pltpu.VMEM)] * 3,
        name="finish",
    )(terms, gains)


def assemble_kernel(parts_ref, out_ref):
    groups, heads = parts_ref.shape[:2]
    for j in range(groups):
        for h in range(heads):
            at = (j * heads + h) * HEAD_DIM
            out_ref[0, :, at : at + HEAD_DIM] = parts_ref[j, h]


def assemble(parts):
    groups, heads, tokens, _ = parts.shape
    rows = min(32, tokens)
    return pl.pallas_call(
        assemble_kernel,
        grid=(tokens // rows,),
        in_specs=[pl.BlockSpec((groups, heads, rows, HEAD_DIM), lambda i: (0, 0, i, 0))],
        out_specs=pl.BlockSpec((1, rows, groups * heads * HEAD_DIM), lambda i: (0, i, 0)),
        out_shape=jax.ShapeDtypeStruct((1, tokens, groups * heads * HEAD_DIM), parts.dtype),
        compiler_params=params(),
        name="assemble",
    )(parts)


def by_step(parts):
    size = len(parts)
    received = list(parts)
    for step in [*range(2, size, 2), *range(3, size, 2), 1]:
        received[step] = swap(parts[step], "seq", step)
    return received


def by_pairs(parts):
    return [parts[0]] + [swap(parts[pair], "seq", 2 * pair) for pair in range(1, len(parts))]


def by_source(stacked):
    return [lax.all_to_all(stacked, "seq", split_axis=0, concat_axis=0, tiled=True)]


def local(
    query_teacher,
    key_teacher,
    value_teacher,
    query_student,
    key_student,
    value_student,
    timesteps,
    student_gain,
    ema_gain,
):
    groups = lax.axis_size("seq")
    clips = lax.axis_size("fsdp")
    tokens = query_teacher.shape[1]
    inner = query_teacher.shape[2]
    width = inner // groups
    heads = width // HEAD_DIM
    split = max(heads - 1, 1) * HEAD_DIM

    sent = prep(query_student[0], key_student[0], value_student[0], groups, width, [(0, width, True)])
    student_parts = by_step(sent)
    sent, later = lax.optimization_barrier((sent, (query_teacher, key_teacher, value_teacher)))
    later = [x[0] for x in later]
    counts = (split // HEAD_DIM, heads - split // HEAD_DIM)
    near = prep_pairs(*later, groups, width, counts, None)
    near, own_gains = lax.optimization_barrier((near, jnp.concatenate([student_gain, ema_gain], axis=0)))
    own_gains = jnp.broadcast_to(own_gains, (clips, *own_gains.shape))
    gains = lax.all_to_all(own_gains, "fsdp", split_axis=0, concat_axis=0, tiled=True)
    near, gains = lax.optimization_barrier((swap(near, "seq", 1), gains))
    sent = prep_pairs(*later, groups, width, counts, near)
    first_sent, second_sent = sent[: groups // 2], sent[groups // 2 :]
    teacher_first = by_pairs(first_sent)
    student_parts, second_sent = lax.optimization_barrier((student_parts, second_sent))
    teacher_second = by_pairs(second_sent)
    out, lse = student(student_parts, gains, groups, tokens, width)
    teacher_first, going = lax.optimization_barrier((teacher_first, out))
    returned = by_source(going)[0]
    grads = teacher(
        timesteps, teacher_first, student_parts, gains, out, lse, None, 0, split // HEAD_DIM, groups, tokens, width, 1
    )
    grads = teacher(
        timesteps,
        teacher_second,
        student_parts,
        gains,
        out,
        lse,
        grads,
        split // HEAD_DIM,
        heads - split // HEAD_DIM,
        groups,
        tokens,
        width,
        clips * groups,
    )
    returned, grads = lax.optimization_barrier((returned, grads))
    student_out = assemble(returned)
    terms = lax.all_to_all(grads, ("fsdp", "seq"), split_axis=0, concat_axis=0, tiled=True)
    loss, gain_grad, new_student, new_ema = finish(terms, gains, groups, student_gain.shape[1])
    return (student_out, loss, gain_grad, new_student, new_ema)


def solution(mesh):
    in_specs = (
        P("fsdp", "seq", None),
        P("fsdp", "seq", None),
        P("fsdp", "seq", None),
        P("fsdp", "seq", None),
        P("fsdp", "seq", None),
        P("fsdp", "seq", None),
        P("fsdp"),
        P(None, "fsdp"),
        P(None, "fsdp"),
    )
    out_specs = (P("fsdp", "seq", None), P("fsdp"), P(None, "fsdp"), P(None, "fsdp"), P())
    return jax.shard_map(local, mesh=mesh, in_specs=in_specs, out_specs=out_specs, check_vma=False)
```

```python
import functools
import math

import jax
import jax.numpy as jnp
from jax import lax
from jax.experimental import pallas as pl
from jax.experimental.pallas import tpu as pltpu
from jax.sharding import PartitionSpec as P

HEAD_DIM = 128
TSTEPS = 50

norm_eps = 1e-06
step_size = 0.01
ema_decay = 0.95

VMEM_BYTES = 60 * 1024 * 1024
STUDENT_BLOCK = 512
TEACHER_BLOCK = 512
TERMS = 4

f32 = jnp.float32
bf16 = jnp.bfloat16


def params(limit=VMEM_BYTES):
    return pltpu.CompilerParams(vmem_limit_bytes=limit)


def cost(flops, nbytes, exps=0):
    return pl.CostEstimate(flops=flops, bytes_accessed=nbytes, transcendentals=exps)


def swap(x, axis, step):
    size = lax.axis_size(axis)
    return lax.ppermute(x, axis, [(i, i ^ step) for i in range(size)])


def nn(a, b):
    return lax.dot_general(a, b, (((1,), (0,)), ((), ())), preferred_element_type=f32)


def prep_kernel(groups, width, plans, *refs):
    ins, outs = refs[:3], refs[3:]
    me = lax.axis_index("seq")
    inverse = []
    for x_ref in ins[:2]:
        wide = x_ref[...].astype(f32)
        inverse.append(lax.rsqrt(jnp.mean(wide * wide, axis=-1, keepdims=True) + norm_eps))

    at = 0
    for first, columns, by_step in plans:
        for slot in range(groups):
            if by_step:
                col = pl.multiple_of((me ^ slot) * width + first, HEAD_DIM)
            else:
                col = slot * width + first
            for a in range(3):
                part = ins[a][:, pl.ds(col, columns)]
                if a < 2:
                    part = (part.astype(f32) * inverse[a]).astype(bf16)
                for h in range(columns // HEAD_DIM):
                    head = part[:, h * HEAD_DIM : (h + 1) * HEAD_DIM]
                    if by_step:
                        outs[at + slot][h, a] = head
                    else:
                        outs[at][slot, h, a] = head
        at += groups if by_step else 1


def prep(q, k, v, groups, width, plans):
    tokens, inner = q.shape
    rows = min(64, tokens)
    shapes, specs = [], []
    for _, columns, by_step in plans:
        heads = columns // HEAD_DIM
        if by_step:
            for _ in range(groups):
                shapes.append(jax.ShapeDtypeStruct((heads, 3, tokens, HEAD_DIM), bf16))
                specs.append(pl.BlockSpec((heads, 3, rows, HEAD_DIM), lambda i: (0, 0, i, 0)))
        else:
            shapes.append(jax.ShapeDtypeStruct((groups, heads, 3, tokens, HEAD_DIM), bf16))
            specs.append(pl.BlockSpec((groups, heads, 3, rows, HEAD_DIM), lambda i: (0, 0, 0, i, 0)))
    return pl.pallas_call(
        functools.partial(prep_kernel, groups, width, plans),
        grid=(tokens // rows,),
        in_specs=[pl.BlockSpec((rows, inner), lambda i: (i, 0))] * 3,
        out_specs=specs,
        out_shape=shapes,
        compiler_params=params(),
        cost_estimate=cost(20 * tokens * inner, 12 * tokens * inner),
        name="prep",
    )(q, k, v)


def scales(refs):
    found = []
    for x_ref in refs:
        wide = x_ref[...].astype(f32)
        found.append(lax.rsqrt(jnp.mean(wide * wide, axis=-1, keepdims=True) + norm_eps))
    return found


def unit_part(ins, inverse, a, col):
    part = ins[a][:, pl.ds(col, HEAD_DIM)]
    return (part.astype(f32) * inverse[a]).astype(bf16) if a < 2 else part


def sibling_kernel(groups, width, *refs):
    ins, out_ref = refs[:3], refs[3]
    me = lax.axis_index("seq")
    inverse = scales(ins[:2])
    for pair in range(groups // 2):
        for h in range(width // HEAD_DIM):
            col = pl.multiple_of((me ^ (2 * pair + 1)) * width + h * HEAD_DIM, HEAD_DIM)
            for a in range(3):
                out_ref[pair, h, a] = unit_part(ins, inverse, a, col)


def pair_kernel(groups, width, counts, *refs):
    ins, near_ref, outs = refs[:3], refs[3], refs[4:]
    me = lax.axis_index("seq")
    inverse = scales(ins[:2])
    at = first = 0
    for count in counts:
        for pair in range(groups // 2):
            for h in range(count):
                col = pl.multiple_of((me ^ (2 * pair)) * width + (first + h) * HEAD_DIM, HEAD_DIM)
                for a in range(3):
                    outs[at + pair][0, h, a] = unit_part(ins, inverse, a, col)
                    outs[at + pair][1, h, a] = near_ref[pair, first + h, a]
        at += groups // 2
        first += count


def prep_pairs(q, k, v, groups, width, counts, near):
    tokens, inner = q.shape
    heads = width // HEAD_DIM
    rows = min(64, tokens)
    in_specs = [pl.BlockSpec((rows, inner), lambda i: (i, 0))] * 3
    near_spec = pl.BlockSpec((groups // 2, heads, 3, rows, HEAD_DIM), lambda i: (0, 0, 0, i, 0))
    near_shape = jax.ShapeDtypeStruct((groups // 2, heads, 3, tokens, HEAD_DIM), bf16)
    if near is None:
        return pl.pallas_call(
            functools.partial(sibling_kernel, groups, width),
            grid=(tokens // rows,),
            in_specs=in_specs,
            out_specs=near_spec,
            out_shape=near_shape,
            compiler_params=params(),
            cost_estimate=cost(20 * tokens * inner, 9 * tokens * inner),
            name="prep_near",
        )(q, k, v)
    shapes, specs = [], []
    for count in counts:
        for _ in range(groups // 2):
            shapes.append(jax.ShapeDtypeStruct((2, count, 3, tokens, HEAD_DIM), bf16))
            specs.append(pl.BlockSpec((2, count, 3, rows, HEAD_DIM), lambda i: (0, 0, 0, i, 0)))
    return pl.pallas_call(
        functools.partial(pair_kernel, groups, width, counts),
        grid=(tokens // rows,),
        in_specs=in_specs + [near_spec],
        out_specs=specs,
        out_shape=shapes,
        compiler_params=params(),
        cost_estimate=cost(20 * tokens * inner, 15 * tokens * inner),
        name="prep_pairs",
    )(q, k, v, near)


def part_at(refs, me, slot, a):
    if refs[0].ndim == 5:
        return refs[slot // 2][slot % 2, 0, a]
    return refs[slot][0, a]


def head_gains(gain_ref, me, width, column):
    own = gain_ref.shape[2]
    tile = (me * width + column) // HEAD_DIM
    tiles = own // HEAD_DIM
    col = pl.multiple_of(lax.rem(tile, tiles) * HEAD_DIM, HEAD_DIM)
    return gain_ref[tile // tiles, :, pl.ds(col, HEAD_DIM)]


def with_gain(unit, gain):
    return (unit.astype(f32) * gain).astype(bf16)


def nt(a, b):
    return lax.dot_general(a, b, (((1,), (1,)), ((), ())), preferred_element_type=f32)


def load(refs, me, groups, tokens, gains, q_scr, k_scr, v_scr):
    for slot in range(groups):
        rows = pl.ds(slot * tokens, tokens)
        q_scr[rows, :] = with_gain(part_at(refs, me, slot, 0), gains[0])
        k_scr[rows, :] = with_gain(part_at(refs, me, slot, 1), gains[1])
        v_scr[rows, :] = part_at(refs, me, slot, 2)


def probabilities(scores):
    factor = HEAD_DIM ** (-0.5) * math.log2(math.e)
    top = jnp.max(scores, axis=-1, keepdims=True)
    raised = jnp.exp2((scores - top) * factor)
    total = jnp.sum(raised, axis=-1, keepdims=True)
    return raised * (1.0 / total), top * factor + jnp.log2(total)


def student_kernel(groups, tokens, width, n_in, *refs):
    ins = refs[:n_in]
    gain_ref, out_ref, lse_ref, q_scr, k_scr, v_scr = refs[n_in:]
    me = lax.axis_index("seq")
    gains = head_gains(gain_ref, me, width, pl.program_id(0) * HEAD_DIM)
    load(ins, me, groups, tokens, (gains[0:1], gains[1:2]), q_scr, k_scr, v_scr)
    length = groups * tokens
    block = min(STUDENT_BLOCK, length)
    scores = nt(q_scr[0:block, :], k_scr[...])
    for start in range(0, length, block):
        rows = pl.ds(start, block)
        later = start + block
        following = nt(q_scr[later : later + block, :], k_scr[...]) if later < length else None
        probs, lse = probabilities(scores)
        scores = following
        out = nn(probs.astype(bf16), v_scr[...]).astype(bf16)
        lse_ref[0, rows, :] = jnp.broadcast_to(lse, (block, HEAD_DIM))
        for j in range(block // tokens):
            out_ref[me ^ (start // tokens + j), 0] = out[j * tokens : (j + 1) * tokens]


def chunk_specs(arrays, groups, tokens, first):
    if arrays[0].ndim == 5:
        return [pl.BlockSpec((2, 1, 3, tokens, HEAD_DIM), lambda h: (0, first + h, 0, 0, 0))] * len(arrays)
    return [pl.BlockSpec((1, 3, tokens, HEAD_DIM), lambda h: (first + h, 0, 0, 0))] * groups


def student(arrays, gains, groups, tokens, width):
    heads = width // HEAD_DIM
    length = groups * tokens
    work = length * length * heads
    return pl.pallas_call(
        functools.partial(student_kernel, groups, tokens, width, len(arrays)),
        grid=(heads,),
        in_specs=chunk_specs(arrays, groups, tokens, 0) + [pl.BlockSpec(gains.shape, lambda h: (0, 0, 0))],
        out_specs=[
            pl.BlockSpec((groups, 1, tokens, HEAD_DIM), lambda h: (0, h, 0, 0)),
            pl.BlockSpec((1, length, HEAD_DIM), lambda h: (h, 0, 0)),
        ],
        out_shape=[
            jax.ShapeDtypeStruct((groups, heads, tokens, HEAD_DIM), bf16),
            jax.ShapeDtypeStruct((heads, length, HEAD_DIM), f32),
        ],
        scratch_shapes=[pltpu.VMEM((length, HEAD_DIM), bf16)] * 3,
        compiler_params=params(),
        cost_estimate=cost(8 * HEAD_DIM * work, 8 * length * width, work),
        name="student",
    )(*arrays, gains)


def teacher_kernel(groups, tokens, width, first, n_teacher, n_student, has_before, *refs):
    step_ref, *refs = refs
    teacher_refs, refs = refs[:n_teacher], refs[n_teacher:]
    student_refs, refs = refs[:n_student], refs[n_student:]
    gain_ref, out_ref, lse_ref, *refs = refs
    if has_before:
        before_ref, *refs = refs
    all_ref, grad_ref, qt, kt, vt, qs, ks, vs = refs
    length = groups * tokens
    block = min(TEACHER_BLOCK, length)
    scale = HEAD_DIM ** (-0.5)
    factor = scale * math.log2(math.e)
    head = pl.program_id(0)
    me = lax.axis_index("seq")
    column = (first + head) * HEAD_DIM
    gains = head_gains(gain_ref, me, width, column)
    load(teacher_refs, me, groups, tokens, (gains[2:3], gains[3:4]), qt, kt, vt)
    load(student_refs, me, groups, tokens, (gains[0:1], gains[1:2]), qs, ks, vs)
    step = jnp.full((1, HEAD_DIM), step_ref[0], jnp.int32).astype(f32)
    weight = 1.0 / (0.05 + (step + 1.0) / TSTEPS)
    share = weight / (length * (groups * width // HEAD_DIM))

    @pl.when(head == 0)
    def _():
        grad_ref[...] = before_ref[...] if has_before else jnp.zeros_like(grad_ref)

    squares = jnp.zeros((1, HEAD_DIM), f32)
    term_q = jnp.zeros((1, HEAD_DIM), f32)
    key_grad = None
    scores = nt(qt[0:block, :], kt[...])
    student_scores = nt(qs[0:block, :], ks[...])
    for start in range(0, length, block):
        rows = pl.ds(start, block)
        slots = range(start // tokens, start // tokens + block // tokens)
        probs, _ = probabilities(scores)
        target = nn(probs.astype(bf16), vt[...]).astype(bf16)
        out = jnp.concatenate([out_ref[me ^ slot, 0] for slot in slots], axis=0)
        diff = out.astype(f32) - target.astype(f32)
        squares = squares + jnp.sum(diff * diff, axis=0, keepdims=True)
        error = (2.0 * share * diff).astype(bf16)
        later = start + block
        if later < length:
            following = nt(qt[later : later + block, :], kt[...]), nt(qs[later : later + block, :], ks[...])
        dprob = nt(error, vs[...])
        lse = jnp.concatenate([lse_ref[0, rows, :]] * (length // HEAD_DIM), axis=1)
        probs = jnp.exp2(student_scores * factor - lse)
        inner = jnp.sum(probs * dprob, axis=-1, keepdims=True)
        dscore = (probs * (dprob - inner)).astype(bf16)
        dquery = (nn(dscore, ks[...]) * scale).astype(bf16)
        unit = jnp.concatenate([part_at(student_refs, me, slot, 0) for slot in slots], axis=0)
        term_q = term_q + jnp.sum(dquery.astype(f32) * unit.astype(f32), axis=0, keepdims=True)
        part = nn(jnp.transpose(qs[rows, :]), dscore)
        key_grad = part if key_grad is None else key_grad + part
        if later < length:
            scores, student_scores = following
    dkey = (jnp.transpose(key_grad) * scale).astype(bf16)
    unit = jnp.concatenate([part_at(student_refs, me, slot, 1) for slot in range(groups)], axis=0)
    term_k = jnp.sum(dkey.astype(f32) * unit.astype(f32), axis=0, keepdims=True)
    cols = pl.ds(pl.multiple_of(column, HEAD_DIM), HEAD_DIM)
    grad_ref[0:1, cols] = term_q
    grad_ref[1:2, cols] = term_k
    grad_ref[2:3, cols] = share * squares

    @pl.when(head == pl.num_programs(0) - 1)
    def _():
        for copy in range(all_ref.shape[0]):
            all_ref[copy] = grad_ref[...]


def teacher(timesteps, arrays, student_arrays, gains, out, lse, before, first, heads, groups, tokens, width, copies):
    length = groups * tokens
    work = length * length * heads
    extra = [] if before is None else [before]
    return pl.pallas_call(
        functools.partial(
            teacher_kernel, groups, tokens, width, first, len(arrays), len(student_arrays), before is not None
        ),
        grid=(heads,),
        in_specs=[pl.BlockSpec(memory_space=pltpu.SMEM)]
        + chunk_specs(arrays, groups, tokens, 0)
        + chunk_specs(student_arrays, groups, tokens, first)
        + [
            pl.BlockSpec(gains.shape, lambda h: (0, 0, 0)),
            pl.BlockSpec((groups, 1, tokens, HEAD_DIM), lambda h: (0, first + h, 0, 0)),
            pl.BlockSpec((1, length, HEAD_DIM), lambda h: (first + h, 0, 0)),
        ]
        + [pl.BlockSpec((None, TERMS, width), lambda h: (0, 0, 0))] * len(extra),
        out_specs=pl.BlockSpec((copies, TERMS, width), lambda h: (0, 0, 0)),
        out_shape=jax.ShapeDtypeStruct((copies, TERMS, width), f32),
        scratch_shapes=[pltpu.VMEM((TERMS, width), f32)] + [pltpu.VMEM((length, HEAD_DIM), bf16)] * 6,
        compiler_params=params(),
        cost_estimate=cost(24 * HEAD_DIM * work, 16 * length * heads * HEAD_DIM, 2 * work),
        name="teacher",
    )(timesteps, *arrays, *student_arrays, gains, out, lse, *extra)


def final_kernel(clips, groups, width, own, terms_ref, gain_ref, loss_ref, grad_ref, student_ref, ema_ref):
    clip = lax.axis_index("fsdp")
    loss = jnp.zeros((1, width), f32)
    terms = []
    for j in range(groups):
        term = terms_ref[j, 0:2, :]
        for other in range(1, clips):
            term = term + terms_ref[other * groups + j, 0:2, :]
        terms.append(term)
        loss = loss + terms_ref[clip * groups + j, 2:3, :]
    loss_ref[0] = jnp.sum(loss)
    for z in range(clips):
        pieces = []
        for j in range(groups):
            low, high = max(j * width, z * own), min((j + 1) * width, (z + 1) * own)
            if low < high:
                pieces.append(terms[j][:, low - j * width : high - j * width])
        term = jnp.concatenate(pieces, axis=1)
        new = gain_ref[z, 0:2, :] - step_size * term
        ema_ref[:, z * own : (z + 1) * own] = ema_decay * gain_ref[z, 2:4, :] + (1.0 - ema_decay) * new

        @pl.when(clip == z)
        def _():
            grad_ref[...] = term
            student_ref[...] = new


def finish(terms, gains, groups, own):
    devices, _, width = terms.shape
    return pl.pallas_call(
        functools.partial(final_kernel, devices // groups, groups, width, own),
        out_shape=[
            jax.ShapeDtypeStruct((1,), f32),
            jax.ShapeDtypeStruct((2, own), f32),
            jax.ShapeDtypeStruct((2, own), f32),
            jax.ShapeDtypeStruct((2, groups * width), f32),
        ],
        out_specs=[pl.BlockSpec(memory_space=pltpu.SMEM)] + [pl.BlockSpec(memory_space=pltpu.VMEM)] * 3,
        name="finish",
    )(terms, gains)


def assemble_kernel(parts_ref, out_ref):
    groups, heads = parts_ref.shape[:2]
    for j in range(groups):
        for h in range(heads):
            at = (j * heads + h) * HEAD_DIM
            out_ref[0, :, at : at + HEAD_DIM] = parts_ref[j, h]


def assemble(parts):
    groups, heads, tokens, _ = parts.shape
    rows = min(32, tokens)
    return pl.pallas_call(
        assemble_kernel,
        grid=(tokens // rows,),
        in_specs=[pl.BlockSpec((groups, heads, rows, HEAD_DIM), lambda i: (0, 0, i, 0))],
        out_specs=pl.BlockSpec((1, rows, groups * heads * HEAD_DIM), lambda i: (0, i, 0)),
        out_shape=jax.ShapeDtypeStruct((1, tokens, groups * heads * HEAD_DIM), parts.dtype),
        compiler_params=params(),
        name="assemble",
    )(parts)


def by_step(parts):
    size = len(parts)
    received = list(parts)
    for step in [*range(2, size, 2), *range(3, size, 2), 1]:
        received[step] = swap(parts[step], "seq", step)
    return received


def by_pairs(parts):
    return [parts[0]] + [swap(parts[pair], "seq", 2 * pair) for pair in range(1, len(parts))]


def by_source(stacked):
    return [lax.all_to_all(stacked, "seq", split_axis=0, concat_axis=0, tiled=True)]


def local(
    query_teacher,
    key_teacher,
    value_teacher,
    query_student,
    key_student,
    value_student,
    timesteps,
    student_gain,
    ema_gain,
):
    groups = lax.axis_size("seq")
    clips = lax.axis_size("fsdp")
    tokens = query_teacher.shape[1]
    inner = query_teacher.shape[2]
    width = inner // groups
    heads = width // HEAD_DIM
    split = (heads + 1) // 2 * HEAD_DIM

    sent = prep(query_student[0], key_student[0], value_student[0], groups, width, [(0, width, True)])
    student_parts = by_step(sent)
    sent, later = lax.optimization_barrier((sent, (query_teacher, key_teacher, value_teacher)))
    later = [x[0] for x in later]
    counts = (split // HEAD_DIM, heads - split // HEAD_DIM)
    near = prep_pairs(*later, groups, width, counts, None)
    near, own_gains = lax.optimization_barrier((near, jnp.concatenate([student_gain, ema_gain], axis=0)))
    own_gains = jnp.broadcast_to(own_gains, (clips, *own_gains.shape))
    gains = lax.all_to_all(own_gains, "fsdp", split_axis=0, concat_axis=0, tiled=True)
    near, gains = lax.optimization_barrier((swap(near, "seq", 1), gains))
    sent = prep_pairs(*later, groups, width, counts, near)
    first_sent, second_sent = sent[: groups // 2], sent[groups // 2 :]
    teacher_first = by_pairs(first_sent)
    ahead, second_sent = lax.optimization_barrier((teacher_first[1], second_sent))
    teacher_first[1] = ahead
    teacher_second = by_pairs(second_sent)
    out, lse = student(student_parts, gains, groups, tokens, width)
    teacher_first, going = lax.optimization_barrier((teacher_first, out))
    returned = by_source(going)[0]
    grads = teacher(
        timesteps, teacher_first, student_parts, gains, out, lse, None, 0, split // HEAD_DIM, groups, tokens, width, 1
    )
    grads = teacher(
        timesteps,
        teacher_second,
        student_parts,
        gains,
        out,
        lse,
        grads,
        split // HEAD_DIM,
        heads - split // HEAD_DIM,
        groups,
        tokens,
        width,
        clips * groups,
    )
    returned, grads = lax.optimization_barrier((returned, grads))
    student_out = assemble(returned)
    terms = lax.all_to_all(grads, ("fsdp", "seq"), split_axis=0, concat_axis=0, tiled=True)
    loss, gain_grad, new_student, new_ema = finish(terms, gains, groups, student_gain.shape[1])
    return (student_out, loss, gain_grad, new_student, new_ema)


def solution(mesh):
    in_specs = (
        P("fsdp", "seq", None),
        P("fsdp", "seq", None),
        P("fsdp", "seq", None),
        P("fsdp", "seq", None),
        P("fsdp", "seq", None),
        P("fsdp", "seq", None),
        P("fsdp"),
        P(None, "fsdp"),
        P(None, "fsdp"),
    )
    out_specs = (P("fsdp", "seq", None), P("fsdp"), P(None, "fsdp"), P(None, "fsdp"), P())
    return jax.shard_map(local, mesh=mesh, in_specs=in_specs, out_specs=out_specs, check_vma=False)
```

```python
import functools
import math

import jax
import jax.numpy as jnp
from jax import lax
from jax.experimental import pallas as pl
from jax.experimental.pallas import tpu as pltpu
from jax.sharding import PartitionSpec as P

HEAD_DIM = 128
TSTEPS = 50

norm_eps = 1e-06
step_size = 0.01
ema_decay = 0.95

VMEM_BYTES = 62 * 1024 * 1024
STUDENT_BLOCK = 512
TEACHER_BLOCK = 512
TERMS = 4
PREP_ROWS = 64

f32 = jnp.float32
bf16 = jnp.bfloat16


def params(limit=VMEM_BYTES):
    return pltpu.CompilerParams(vmem_limit_bytes=limit)


def cost(flops, nbytes, exps=0):
    return pl.CostEstimate(flops=flops, bytes_accessed=nbytes, transcendentals=exps)


def swap(x, axis, step):
    size = lax.axis_size(axis)
    return lax.ppermute(x, axis, [(i, i ^ step) for i in range(size)])


def nn(a, b):
    return lax.dot_general(a, b, (((1,), (0,)), ((), ())), preferred_element_type=f32)


def scales(refs):
    found = []
    for x_ref in refs:
        wide = x_ref[...].astype(f32)
        found.append(lax.rsqrt(jnp.mean(wide * wide, axis=-1, keepdims=True) + norm_eps))
    return found


def unit_part(ins, inverse, a, col):
    part = ins[a][:, pl.ds(col, HEAD_DIM)]
    return (part.astype(f32) * inverse[a]).astype(bf16) if a < 2 else part


def prep_kernel(groups, width, *refs):
    student_ins, teacher_ins, outs, near_ref = refs[:3], refs[3:6], refs[6:-1], refs[-1]
    me = lax.axis_index("seq")
    inverse = scales(student_ins[:2])
    for slot in range(groups):
        for h in range(width // HEAD_DIM):
            col = pl.multiple_of((me ^ slot) * width + h * HEAD_DIM, HEAD_DIM)
            for a in range(3):
                outs[slot][h, a] = unit_part(student_ins, inverse, a, col)
    inverse = scales(teacher_ins[:2])
    for pair in range(groups // 2):
        for h in range(width // HEAD_DIM):
            col = pl.multiple_of((me ^ (2 * pair + 1)) * width + h * HEAD_DIM, HEAD_DIM)
            for a in range(3):
                near_ref[pair, h, a] = unit_part(teacher_ins, inverse, a, col)


def prep(student_ins, teacher_ins, groups, width):
    tokens, inner = student_ins[0].shape
    heads = width // HEAD_DIM
    rows = min(PREP_ROWS, tokens)
    return pl.pallas_call(
        functools.partial(prep_kernel, groups, width),
        grid=(tokens // rows,),
        in_specs=[pl.BlockSpec((rows, inner), lambda i: (i, 0))] * 6,
        out_specs=[pl.BlockSpec((heads, 3, rows, HEAD_DIM), lambda i: (0, 0, i, 0))] * groups
        + [pl.BlockSpec((groups // 2, heads, 3, rows, HEAD_DIM), lambda i: (0, 0, 0, i, 0))],
        out_shape=[jax.ShapeDtypeStruct((heads, 3, tokens, HEAD_DIM), bf16)] * groups
        + [jax.ShapeDtypeStruct((groups // 2, heads, 3, tokens, HEAD_DIM), bf16)],
        compiler_params=params(),
        cost_estimate=cost(40 * tokens * inner, 21 * tokens * inner),
        name="prep",
    )(*student_ins, *teacher_ins)


def pair_kernel(groups, width, counts, *refs):
    ins, near_ref, outs = refs[:3], refs[3], refs[4:]
    me = lax.axis_index("seq")
    inverse = scales(ins[:2])
    at = first = 0
    for count in counts:
        for pair in range(groups // 2):
            for h in range(count):
                col = pl.multiple_of((me ^ (2 * pair)) * width + (first + h) * HEAD_DIM, HEAD_DIM)
                for a in range(3):
                    outs[at + pair][0, h, a] = unit_part(ins, inverse, a, col)
                    outs[at + pair][1, h, a] = near_ref[pair, first + h, a]
        at += groups // 2
        first += count


def prep_pairs(q, k, v, groups, width, counts, near):
    tokens, inner = q.shape
    heads = width // HEAD_DIM
    rows = min(PREP_ROWS, tokens)
    in_specs = [pl.BlockSpec((rows, inner), lambda i: (i, 0))] * 3
    near_spec = pl.BlockSpec((groups // 2, heads, 3, rows, HEAD_DIM), lambda i: (0, 0, 0, i, 0))
    shapes, specs = [], []
    for count in counts:
        for _ in range(groups // 2):
            shapes.append(jax.ShapeDtypeStruct((2, count, 3, tokens, HEAD_DIM), bf16))
            specs.append(pl.BlockSpec((2, count, 3, rows, HEAD_DIM), lambda i: (0, 0, 0, i, 0)))
    return pl.pallas_call(
        functools.partial(pair_kernel, groups, width, counts),
        grid=(tokens // rows,),
        in_specs=in_specs + [near_spec],
        out_specs=specs,
        out_shape=shapes,
        compiler_params=params(),
        cost_estimate=cost(20 * tokens * inner, 15 * tokens * inner),
        name="prep_pairs",
    )(q, k, v, near)


def part_at(refs, me, slot, a):
    if refs[0].ndim == 5:
        return refs[slot // 2][slot % 2, 0, a]
    return refs[slot][0, a]


def head_gains(gain_ref, me, width, column):
    own = gain_ref.shape[2]
    tile = (me * width + column) // HEAD_DIM
    tiles = own // HEAD_DIM
    col = pl.multiple_of(lax.rem(tile, tiles) * HEAD_DIM, HEAD_DIM)
    return gain_ref[tile // tiles, :, pl.ds(col, HEAD_DIM)]


def with_gain(unit, gain):
    return (unit.astype(f32) * gain).astype(bf16)


def nt(a, b):
    return lax.dot_general(a, b, (((1,), (1,)), ((), ())), preferred_element_type=f32)


def load(refs, me, groups, tokens, gains, q_scr, k_scr, v_scr):
    for slot in range(groups):
        rows = pl.ds(slot * tokens, tokens)
        q_scr[rows, :] = with_gain(part_at(refs, me, slot, 0), gains[0])
        k_scr[rows, :] = with_gain(part_at(refs, me, slot, 1), gains[1])
        v_scr[rows, :] = part_at(refs, me, slot, 2)


def probabilities(scores):
    factor = HEAD_DIM ** (-0.5) * math.log2(math.e)
    top = jnp.max(scores, axis=-1, keepdims=True)
    raised = jnp.exp2((scores - top) * factor)
    total = jnp.sum(raised, axis=-1, keepdims=True)
    return raised * (1.0 / total), top * factor + jnp.log2(total)


def student_kernel(groups, tokens, width, n_in, *refs):
    ins = refs[:n_in]
    gain_ref, out_ref, lse_ref, q_scr, k_scr, v_scr = refs[n_in:]
    me = lax.axis_index("seq")
    gains = head_gains(gain_ref, me, width, pl.program_id(0) * HEAD_DIM)
    load(ins, me, groups, tokens, (gains[0:1], gains[1:2]), q_scr, k_scr, v_scr)
    length = groups * tokens
    block = min(STUDENT_BLOCK, length)
    scores = nt(q_scr[0:block, :], k_scr[...])
    for start in range(0, length, block):
        rows = pl.ds(start, block)
        later = start + block
        following = nt(q_scr[later : later + block, :], k_scr[...]) if later < length else None
        probs, lse = probabilities(scores)
        scores = following
        out = nn(probs.astype(bf16), v_scr[...]).astype(bf16)
        lse_ref[0, rows, :] = jnp.broadcast_to(lse, (block, HEAD_DIM))
        for j in range(block // tokens):
            out_ref[me ^ (start // tokens + j), 0] = out[j * tokens : (j + 1) * tokens]


def chunk_specs(arrays, groups, tokens, first):
    if arrays[0].ndim == 5:
        return [pl.BlockSpec((2, 1, 3, tokens, HEAD_DIM), lambda h: (0, first + h, 0, 0, 0))] * len(arrays)
    return [pl.BlockSpec((1, 3, tokens, HEAD_DIM), lambda h: (first + h, 0, 0, 0))] * groups


def student(arrays, gains, groups, tokens, width):
    heads = width // HEAD_DIM
    length = groups * tokens
    work = length * length * heads
    return pl.pallas_call(
        functools.partial(student_kernel, groups, tokens, width, len(arrays)),
        grid=(heads,),
        in_specs=chunk_specs(arrays, groups, tokens, 0) + [pl.BlockSpec(gains.shape, lambda h: (0, 0, 0))],
        out_specs=[
            pl.BlockSpec((groups, 1, tokens, HEAD_DIM), lambda h: (0, h, 0, 0)),
            pl.BlockSpec((1, length, HEAD_DIM), lambda h: (h, 0, 0)),
        ],
        out_shape=[
            jax.ShapeDtypeStruct((groups, heads, tokens, HEAD_DIM), bf16),
            jax.ShapeDtypeStruct((heads, length, HEAD_DIM), f32),
        ],
        scratch_shapes=[pltpu.VMEM((length, HEAD_DIM), bf16)] * 3,
        compiler_params=params(),
        cost_estimate=cost(8 * HEAD_DIM * work, 8 * length * width, work),
        name="student",
    )(*arrays, gains)


def teacher_kernel(groups, tokens, width, first, n_teacher, n_student, has_before, *refs):
    step_ref, *refs = refs
    teacher_refs, refs = refs[:n_teacher], refs[n_teacher:]
    student_refs, refs = refs[:n_student], refs[n_student:]
    gain_ref, out_ref, lse_ref, *refs = refs
    if has_before:
        before_ref, *refs = refs
    all_ref, grad_ref, qt, kt, vt, qs, ks, vs = refs
    length = groups * tokens
    block = min(TEACHER_BLOCK, length)
    scale = HEAD_DIM ** (-0.5)
    factor = scale * math.log2(math.e)
    head = pl.program_id(0)
    me = lax.axis_index("seq")
    column = (first + head) * HEAD_DIM
    gains = head_gains(gain_ref, me, width, column)
    load(teacher_refs, me, groups, tokens, (gains[2:3], gains[3:4]), qt, kt, vt)
    load(student_refs, me, groups, tokens, (gains[0:1], gains[1:2]), qs, ks, vs)
    step = jnp.full((1, HEAD_DIM), step_ref[0], jnp.int32).astype(f32)
    weight = 1.0 / (0.05 + (step + 1.0) / TSTEPS)
    share = weight / (length * (groups * width // HEAD_DIM))

    @pl.when(head == 0)
    def _():
        grad_ref[...] = before_ref[...] if has_before else jnp.zeros_like(grad_ref)

    squares = jnp.zeros((1, HEAD_DIM), f32)
    term_q = jnp.zeros((1, HEAD_DIM), f32)
    key_grad = None
    scores = nt(qt[0:block, :], kt[...])
    student_scores = nt(qs[0:block, :], ks[...])
    for start in range(0, length, block):
        rows = pl.ds(start, block)
        slots = range(start // tokens, start // tokens + block // tokens)
        probs, _ = probabilities(scores)
        target = nn(probs.astype(bf16), vt[...]).astype(bf16)
        out = jnp.concatenate([out_ref[me ^ slot, 0] for slot in slots], axis=0)
        diff = out.astype(f32) - target.astype(f32)
        squares = squares + jnp.sum(diff * diff, axis=0, keepdims=True)
        error = (2.0 * share * diff).astype(bf16)
        later = start + block
        if later < length:
            following = nt(qt[later : later + block, :], kt[...]), nt(qs[later : later + block, :], ks[...])
        dprob = nt(error, vs[...])
        lse = jnp.concatenate([lse_ref[0, rows, :]] * (length // HEAD_DIM), axis=1)
        probs = jnp.exp2(student_scores * factor - lse)
        inner = jnp.sum(probs * dprob, axis=-1, keepdims=True)
        dscore = (probs * (dprob - inner)).astype(bf16)
        dquery = (nn(dscore, ks[...]) * scale).astype(bf16)
        unit = jnp.concatenate([part_at(student_refs, me, slot, 0) for slot in slots], axis=0)
        term_q = term_q + jnp.sum(dquery.astype(f32) * unit.astype(f32), axis=0, keepdims=True)
        part = nn(jnp.transpose(qs[rows, :]), dscore)
        key_grad = part if key_grad is None else key_grad + part
        if later < length:
            scores, student_scores = following
    dkey = (jnp.transpose(key_grad) * scale).astype(bf16)
    unit = jnp.concatenate([part_at(student_refs, me, slot, 1) for slot in range(groups)], axis=0)
    term_k = jnp.sum(dkey.astype(f32) * unit.astype(f32), axis=0, keepdims=True)
    cols = pl.ds(pl.multiple_of(column, HEAD_DIM), HEAD_DIM)
    grad_ref[0:1, cols] = term_q
    grad_ref[1:2, cols] = term_k
    grad_ref[2:3, cols] = share * squares

    @pl.when(head == pl.num_programs(0) - 1)
    def _():
        for copy in range(all_ref.shape[0]):
            all_ref[copy] = grad_ref[...]


def teacher(timesteps, arrays, student_arrays, gains, out, lse, before, first, heads, groups, tokens, width, copies):
    length = groups * tokens
    work = length * length * heads
    extra = [] if before is None else [before]
    return pl.pallas_call(
        functools.partial(
            teacher_kernel, groups, tokens, width, first, len(arrays), len(student_arrays), before is not None
        ),
        grid=(heads,),
        in_specs=[pl.BlockSpec(memory_space=pltpu.SMEM)]
        + chunk_specs(arrays, groups, tokens, 0)
        + chunk_specs(student_arrays, groups, tokens, first)
        + [
            pl.BlockSpec(gains.shape, lambda h: (0, 0, 0)),
            pl.BlockSpec((groups, 1, tokens, HEAD_DIM), lambda h: (0, first + h, 0, 0)),
            pl.BlockSpec((1, length, HEAD_DIM), lambda h: (first + h, 0, 0)),
        ]
        + [pl.BlockSpec((None, TERMS, width), lambda h: (0, 0, 0))] * len(extra),
        out_specs=pl.BlockSpec((copies, TERMS, width), lambda h: (0, 0, 0)),
        out_shape=jax.ShapeDtypeStruct((copies, TERMS, width), f32),
        scratch_shapes=[pltpu.VMEM((TERMS, width), f32)] + [pltpu.VMEM((length, HEAD_DIM), bf16)] * 6,
        compiler_params=params(),
        cost_estimate=cost(24 * HEAD_DIM * work, 16 * length * heads * HEAD_DIM, 2 * work),
        name="teacher",
    )(timesteps, *arrays, *student_arrays, gains, out, lse, *extra)


def final_kernel(clips, groups, width, own, terms_ref, gain_ref, loss_ref, grad_ref, student_ref, ema_ref):
    clip = lax.axis_index("fsdp")
    loss = jnp.zeros((1, width), f32)
    terms = []
    for j in range(groups):
        term = terms_ref[j, 0:2, :]
        for other in range(1, clips):
            term = term + terms_ref[other * groups + j, 0:2, :]
        terms.append(term)
        loss = loss + terms_ref[clip * groups + j, 2:3, :]
    loss_ref[0] = jnp.sum(loss)
    for z in range(clips):
        pieces = []
        for j in range(groups):
            low, high = max(j * width, z * own), min((j + 1) * width, (z + 1) * own)
            if low < high:
                pieces.append(terms[j][:, low - j * width : high - j * width])
        term = jnp.concatenate(pieces, axis=1)
        new = gain_ref[z, 0:2, :] - step_size * term
        ema_ref[:, z * own : (z + 1) * own] = ema_decay * gain_ref[z, 2:4, :] + (1.0 - ema_decay) * new

        @pl.when(clip == z)
        def _():
            grad_ref[...] = term
            student_ref[...] = new


def finish(terms, gains, groups, own):
    devices, _, width = terms.shape
    return pl.pallas_call(
        functools.partial(final_kernel, devices // groups, groups, width, own),
        out_shape=[
            jax.ShapeDtypeStruct((1,), f32),
            jax.ShapeDtypeStruct((2, own), f32),
            jax.ShapeDtypeStruct((2, own), f32),
            jax.ShapeDtypeStruct((2, groups * width), f32),
        ],
        out_specs=[pl.BlockSpec(memory_space=pltpu.SMEM)] + [pl.BlockSpec(memory_space=pltpu.VMEM)] * 3,
        name="finish",
    )(terms, gains)


def assemble_kernel(parts_ref, out_ref):
    groups, heads = parts_ref.shape[:2]
    for j in range(groups):
        for h in range(heads):
            at = (j * heads + h) * HEAD_DIM
            out_ref[0, :, at : at + HEAD_DIM] = parts_ref[j, h]


def assemble(parts):
    groups, heads, tokens, _ = parts.shape
    rows = min(32, tokens)
    return pl.pallas_call(
        assemble_kernel,
        grid=(tokens // rows,),
        in_specs=[pl.BlockSpec((groups, heads, rows, HEAD_DIM), lambda i: (0, 0, i, 0))],
        out_specs=pl.BlockSpec((1, rows, groups * heads * HEAD_DIM), lambda i: (0, i, 0)),
        out_shape=jax.ShapeDtypeStruct((1, tokens, groups * heads * HEAD_DIM), parts.dtype),
        compiler_params=params(),
        name="assemble",
    )(parts)


def chunk_heads(heads):
    return (heads - heads // 2, heads // 2) if heads > 1 else (1,)


def by_step(parts):
    size = len(parts)
    received = list(parts)
    for step in [*range(2, size, 2), *range(3, size, 2), 1]:
        received[step] = swap(parts[step], "seq", step)
    return received


def by_pairs(parts):
    return [parts[0]] + [swap(parts[pair], "seq", 2 * pair) for pair in range(1, len(parts))]


def by_source(stacked):
    return [lax.all_to_all(stacked, "seq", split_axis=0, concat_axis=0, tiled=True)]


def local(
    query_teacher,
    key_teacher,
    value_teacher,
    query_student,
    key_student,
    value_student,
    timesteps,
    student_gain,
    ema_gain,
):
    groups = lax.axis_size("seq")
    clips = lax.axis_size("fsdp")
    tokens = query_teacher.shape[1]
    inner = query_teacher.shape[2]
    width = inner // groups
    heads = width // HEAD_DIM

    later = [query_teacher[0], key_teacher[0], value_teacher[0]]
    counts = chunk_heads(heads)
    *sent, near = prep([query_student[0], key_student[0], value_student[0]], later, groups, width)
    student_parts = by_step(sent)
    near, *own_gains = lax.optimization_barrier((near, student_gain, ema_gain))
    own_gains = jnp.concatenate(own_gains, axis=0)
    own_gains = jnp.broadcast_to(own_gains, (clips, *own_gains.shape))
    gains = lax.all_to_all(own_gains, "fsdp", split_axis=0, concat_axis=0, tiled=True)
    near, gains = lax.optimization_barrier((swap(near, "seq", 1), gains))
    sent = prep_pairs(*later, groups, width, counts, near)
    pairs = groups // 2
    chunks = [by_pairs(sent[:pairs])]
    for i in range(1, len(counts)):
        ahead, going = lax.optimization_barrier((chunks[-1][1], sent[i * pairs : (i + 1) * pairs]))
        chunks[-1][1] = ahead
        chunks.append(by_pairs(going))
    out, lse = student(student_parts, gains, groups, tokens, width)
    chunks[0], going = lax.optimization_barrier((chunks[0], out))
    returned = by_source(going)[0]
    grads, first = None, 0
    for i, count in enumerate(counts):
        copies = clips * groups if i == len(counts) - 1 else 1
        grads = teacher(
            timesteps, chunks[i], student_parts, gains, out, lse, grads, first, count, groups, tokens, width, copies
        )
        first += count
    returned, grads = lax.optimization_barrier((returned, grads))
    student_out = assemble(returned)
    terms = lax.all_to_all(grads, ("fsdp", "seq"), split_axis=0, concat_axis=0, tiled=True)
    loss, gain_grad, new_student, new_ema = finish(terms, gains, groups, student_gain.shape[1])
    return (student_out, loss, gain_grad, new_student, new_ema)


def solution(mesh):
    in_specs = (
        P("fsdp", "seq", None),
        P("fsdp", "seq", None),
        P("fsdp", "seq", None),
        P("fsdp", "seq", None),
        P("fsdp", "seq", None),
        P("fsdp", "seq", None),
        P("fsdp"),
        P(None, "fsdp"),
        P(None, "fsdp"),
    )
    out_specs = (P("fsdp", "seq", None), P("fsdp"), P(None, "fsdp"), P(None, "fsdp"), P())
    return jax.shard_map(local, mesh=mesh, in_specs=in_specs, out_specs=out_specs, check_vma=False)
```
